32 devices in a mesh: replica: 8 (over y, x, core), fsdp: 4 (over z).
Axes of the slice: x: 2, y: 2, z: 4, core: 2. Of those that a mesh axis runs over, the one named last changes fastest.
Arguments:
- acts: bfloat16 [4096, 5120], P(('replica', 'fsdp')), may hold values from -6 to 6
- cotangent: bfloat16 [4096, 384], P(('replica', 'fsdp')), may hold values from -6 to 6
- inner_weight: bfloat16 [5120, 384], P('fsdp'), may hold values from -1.5 to 1.5
- outer_weight: float32 [5120, 384], P('fsdp'), may hold values from -1.5 to 1.5
- momentum: float32 [5120, 384], P('fsdp'), may hold values from -1.5 to 1.5
Outputs:
- input_grad: bfloat16 [4096, 5120], P(('replica', 'fsdp'))
- new_outer: float32 [5120, 384], P('fsdp')
- new_momentum: float32 [5120, 384], P('fsdp')
- new_inner: bfloat16 [5120, 384], P('fsdp')
The draws below stay inside these ranges and needn't reach their ends.
All inputs are finite; a program needn't handle non-finite values.
Results may differ from the reference program's by a relative error of at most 0.015.
Values may be sent and summed in bfloat16 or wider, within the bound.
A program may use at most 64 MiB of HBM per device.

```python
import jax
import jax.numpy as jnp
from jax import lax

D = 5120
P_SIZE = 384
TOK_DEV = 128
TOKENS = 4096
N_REPLICA = 8
N_FSDP = 4


def level_of(key, shape, pieces, smallest, largest):
    def one(position, parts):
        draws = jax.random.uniform(jax.random.fold_in(jax.random.fold_in(key, 6), position), (parts,), jnp.float32, smallest / len(pieces), largest / len(pieces))
        return jnp.repeat(jnp.exp(draws), shape[position] // parts).reshape((-1,) + (1,) * (len(shape) - position - 1))

    factor_of = one(*pieces[0])
    for cut in pieces[1:]:
        factor_of = factor_of * one(*cut)
    return factor_of


def gaussian(key, dims, scale, bound, cuts=(), dtype=jnp.bfloat16):
    gain = level_of(key, dims, cuts, -0.22, 0.18) if cuts else 1.0
    drawn = jax.random.normal(key, dims, jnp.float32) * scale * gain
    return jnp.minimum(jnp.maximum(drawn, -bound), bound).astype(dtype)


def setup_inputs(seed: int = 0) -> dict:
    seeds = jax.random.split(jax.random.key(seed), 6)
    return {
        "acts": gaussian(seeds[0], (TOKENS, D), 1.0, 6.0, ((0, 32),)),
        "cotangent": gaussian(seeds[1], (TOKENS, P_SIZE), 1.0, 6.0, ((0, 32),)),
        "inner_weight": gaussian(seeds[2], (D, P_SIZE), 0.25, 1.5, ((0, 4),)),
        "outer_weight": gaussian(seeds[3], (D, P_SIZE), 0.25, 1.5, ((0, 4),), jnp.float32),
        "momentum": gaussian(seeds[4], (D, P_SIZE), 0.25, 1.5, ((0, 4),), jnp.float32),
    }


lr_inner = 4.0
beta = 0.9
lr_outer = 0.7


def reference(acts, cotangent, inner_weight, outer_weight, momentum):
    scale = 1.0 / (D ** 0.5)
    xs = acts.reshape(N_REPLICA, N_FSDP * TOK_DEV, D)
    gs = cotangent.reshape(N_REPLICA, N_FSDP * TOK_DEV, P_SIZE)
    wfl = inner_weight.astype(jnp.float32)

    def per_replica(carry, inputs):
        x_rows, g_rows = inputs
        pre = jnp.dot(x_rows, inner_weight, preferred_element_type=jnp.float32) * scale
        sig = jax.nn.sigmoid(pre)
        grad_pre = (g_rows.astype(jnp.float32) * sig * (1.0 + pre * (1.0 - sig))).astype(jnp.bfloat16)
        input_grad = (jnp.dot(grad_pre, inner_weight.T, preferred_element_type=jnp.float32) * scale).astype(jnp.bfloat16)
        xg = x_rows.reshape(N_FSDP, TOK_DEV, D).astype(jnp.float32)
        gg = grad_pre.reshape(N_FSDP, TOK_DEV, P_SIZE).astype(jnp.float32)
        terms = (jnp.einsum('ftd,ftp->fdp', xg, gg) * scale).astype(jnp.bfloat16).astype(jnp.float32)
        weight_grad = jnp.sum(terms, axis=0)
        delta = outer_weight - (wfl - lr_inner * weight_grad)
        return carry + delta, input_grad

    total, grads = lax.scan(per_replica, jnp.zeros((D, P_SIZE), jnp.float32), (xs, gs))
    mean_delta = total / N_REPLICA
    new_momentum = beta * momentum + mean_delta
    new_outer = outer_weight - lr_outer * (mean_delta + beta * new_momentum)
    return grads.reshape(TOKENS, D), new_outer, new_momentum, new_outer.astype(jnp.bfloat16)
```

```python
import functools

import jax
import jax.numpy as jnp
from jax import lax
from jax.experimental import pallas as pl
from jax.experimental.pallas import tpu as pltpu
from jax.sharding import PartitionSpec as P

lr_inner = 4.0
beta = 0.9
lr_outer = 0.7

MESH = pl.DeviceIdType.MESH


def contract_rows(left, right):
    return lax.dot_general(
        left, right, (((0,), (0,)), ((), ())), preferred_element_type=jnp.float32
    )


def outer_update(delta_mean, outer_rows, moment_rows):
    moment_next = beta * moment_rows + delta_mean
    outer_next = outer_rows - lr_outer * (delta_mean + beta * moment_next)
    return (outer_next, moment_next)


def kernel(
    n_fsdp,
    acts_hbm,
    cot_hbm,
    w_hbm,
    ig_hbm,
    g_hbm,
    acts,
    cot,
    acts_t,
    w_all,
    ig,
    sib_out,
    sib_in,
    half_sum,
    plane_in,
    shard_out,
    shard_in,
    total,
    local_sem,
    wz_s,
    wz_r,
    wp_s,
    wp_r,
    wc_s,
    wc_r,
    tc_s,
    tc_r,
    tp_s,
    tp_r,
    tz_s,
    tz_r,
    gp_s,
    gp_r,
    gc_s,
    gc_r,
):
    me = lax.axis_index("replica")
    z = lax.axis_index("fsdp")
    rows = w_hbm.shape[0]
    half = rows // 2
    sub = half // 4
    width = acts.shape[1]
    scale = 1.0 / width**0.5
    chip, core = me // 2, me % 2
    x, y = chip % 2, chip // 2
    chips = ((1 - y) * 2 + 1 - x, y * 2 + 1 - x, (1 - y) * 2 + x)
    sibling = (chip * 2 + 1 - core, z)
    peers = [(q * 2 + core, z) for q in chips]
    steps = range(1, n_fsdp)
    above = [(z + j) % n_fsdp for j in range(n_fsdp)]
    below = [(z + n_fsdp - j) % n_fsdp for j in range(n_fsdp)]

    def at(ref, start, size):
        return ref.at[pl.ds(pl.multiple_of(start, 16), size)]

    def remote(src, dst, s, r, dev):
        return pltpu.make_async_remote_copy(
            src_ref=src, dst_ref=dst, send_sem=s, recv_sem=r, device_id=dev, device_id_type=MESH
        )

    loads = [
        pltpu.make_async_copy(w_hbm, at(w_all, z * rows, rows), local_sem.at[0]),
        pltpu.make_async_copy(acts_hbm, acts, local_sem.at[1]),
        pltpu.make_async_copy(cot_hbm, cot, local_sem.at[2]),
    ]
    for load in loads:
        load.start()

    barrier = pltpu.get_barrier_semaphore()
    partners = [(me, above[j]) for j in steps] + peers + [sibling]
    for dev in partners:
        pl.semaphore_signal(barrier, inc=1, device_id=dev, device_id_type=MESH)
    pl.semaphore_wait(barrier, len(partners))

    sent = []

    def send(src, dst, s, r, dev):
        copy = remote(src, dst, s, r, dev)
        copy.start()
        sent.append(copy)

    def arrived(landing, s, r, dev):
        remote(landing, landing, s, r, dev).wait_recv()

    mine = core * half + chip * sub
    for j in steps:
        send(
            at(w_hbm, mine, sub),
            at(w_all, z * rows + mine, sub),
            wz_s.at[j - 1],
            wz_r.at[j - 1],
            (me, above[j]),
        )
    for load in loads:
        load.wait()

    def partial_pre(start, size):
        start = pl.multiple_of(start, 128)
        return jnp.dot(
            acts[:, pl.ds(start, size)],
            w_all[pl.ds(start, size), :],
            preferred_element_type=jnp.float32,
        )

    for j in steps:
        piece = at(w_all, below[j] * rows + mine, sub)
        arrived(piece, wz_s.at[j - 1], wz_r.at[j - 1], (me, above[j]))
        for k in range(3):
            send(piece, piece, wp_s.at[j - 1, k], wp_r.at[j - 1, k], peers[k])

    pre = partial_pre(z * rows, rows)
    for b in range(width // half):
        acts_t[b * half : (b + 1) * half, :] = acts[:, b * half : (b + 1) * half].T

    for j in steps:
        start = below[j] * rows + core * half
        for k in range(3):
            piece = at(w_all, start + chips[k] * sub, sub)
            arrived(piece, wp_s.at[j - 1, k], wp_r.at[j - 1, k], peers[k])
        piece = at(w_all, start, half)
        send(piece, piece, wc_s.at[j - 1], wc_r.at[j - 1], sibling)
        pre += partial_pre(start, half)
    for j in steps:
        start = below[j] * rows + (1 - core) * half
        arrived(at(w_all, start, half), wc_s.at[j - 1], wc_r.at[j - 1], sibling)
        pre += partial_pre(start, half)

    pre = pre * scale
    sig = jax.nn.sigmoid(pre)
    grad_pre = (cot[...].astype(jnp.float32) * sig * (1.0 + pre * (1.0 - sig))).astype(
        jnp.bfloat16
    )

    def term(start):
        block = acts_t[pl.ds(pl.multiple_of(start, 128), half), :]
        return jnp.dot(block, grad_pre, preferred_element_type=jnp.float32) * scale

    order = [j % n_fsdp for j in range(1, n_fsdp + 1)]
    for i, j in enumerate(order):
        sib_out[i] = term(above[j] * rows + (1 - core) * half).astype(jnp.bfloat16)
        send(sib_out.at[i], sib_in.at[i], tc_s.at[i], tc_r.at[i], sibling)
    for i, j in enumerate(order):
        own = term(above[j] * rows + core * half)
        arrived(sib_in.at[i], tc_s.at[i], tc_r.at[i], sibling)
        half_sum[i] = (own + sib_in[i].astype(jnp.float32)).astype(jnp.bfloat16)
        for k in range(3):
            send(
                at(half_sum.at[i], chips[k] * sub, sub),
                plane_in.at[i, k],
                tp_s.at[i, k],
                tp_r.at[i, k],
                peers[k],
            )
    stores = []
    for i, j in enumerate(order):
        c0, c1 = i * rows, (i + 1) * rows
        ig[:, c0:c1] = (
            lax.dot_general(
                grad_pre,
                w_all[c0:c1, :],
                (((1,), (1,)), ((), ())),
                preferred_element_type=jnp.float32,
            )
            * scale
        ).astype(jnp.bfloat16)
        store = pltpu.make_async_copy(
            ig.at[:, c0:c1], ig_hbm.at[:, c0:c1], local_sem.at[3 + i]
        )
        store.start()
        stores.append(store)
        acc = half_sum[i, pl.ds(pl.multiple_of(chip * sub, 16), sub), :].astype(jnp.float32)
        for k in range(3):
            arrived(plane_in.at[i, k], tp_s.at[i, k], tp_r.at[i, k], peers[k])
            acc += plane_in[i, k].astype(jnp.float32)
        if j:
            shard_out[i] = acc.astype(jnp.bfloat16)
            send(shard_out.at[i], shard_in.at[i], tz_s.at[i], tz_r.at[i], (me, above[j]))
    for i in range(n_fsdp - 1):
        arrived(shard_in.at[i], tz_s.at[i], tz_r.at[i], (me, above[order[i]]))
        acc += shard_in[i].astype(jnp.float32)

    total[pl.ds(pl.multiple_of(mine, 16), sub), :] = acc.astype(jnp.bfloat16)
    piece = at(total, mine, sub)
    for k in range(3):
        send(piece, piece, gp_s.at[k], gp_r.at[k], peers[k])
    send(piece, piece, gc_s.at[3], gc_r.at[3], sibling)
    for k in (1, 2, 0):
        piece = at(total, core * half + chips[k] * sub, sub)
        arrived(piece, gp_s.at[k], gp_r.at[k], peers[k])
        send(piece, piece, gc_s.at[k], gc_r.at[k], sibling)
    for k in (3, 1, 2, 0):
        q = chip if k == 3 else chips[k]
        arrived(at(total, (1 - core) * half + q * sub, sub), gc_s.at[k], gc_r.at[k], sibling)
    last = pltpu.make_async_copy(total, g_hbm, local_sem.at[3 + n_fsdp])
    last.start()
    for copy in sent:
        copy.wait_send()
    for store in stores:
        store.wait()
    last.wait()


def fused(acts, cotangent, inner_weight, n_fsdp):
    tok, width = acts.shape
    rows, cols = inner_weight.shape
    half, sub = rows // 2, rows // 8
    bf = jnp.bfloat16
    dma = pltpu.SemaphoreType.DMA
    s = n_fsdp - 1
    anywhere = pl.BlockSpec(memory_space=pl.ANY)
    return pl.pallas_call(
        functools.partial(kernel, n_fsdp),
        out_shape=(
            jax.ShapeDtypeStruct((tok, width), bf),
            jax.ShapeDtypeStruct((rows, cols), bf),
        ),
        in_specs=[anywhere] * 3,
        out_specs=(anywhere, anywhere),
        scratch_shapes=[
            pltpu.VMEM((tok, width), bf),
            pltpu.VMEM((tok, cols), bf),
            pltpu.VMEM((width, tok), bf),
            pltpu.VMEM((width, cols), bf),
            pltpu.VMEM((tok, width), bf),
            pltpu.VMEM((n_fsdp, half, cols), bf),
            pltpu.VMEM((n_fsdp, half, cols), bf),
            pltpu.VMEM((n_fsdp, half, cols), bf),
            pltpu.VMEM((n_fsdp, 3, sub, cols), bf),
            pltpu.VMEM((s, sub, cols), bf),
            pltpu.VMEM((s, sub, cols), bf),
            pltpu.VMEM((rows, cols), bf),
            dma((4 + n_fsdp,)),
            dma((s,)),
            dma((s,)),
            dma((s, 3)),
            dma((s, 3)),
            dma((s,)),
            dma((s,)),
            dma((n_fsdp,)),
            dma((n_fsdp,)),
            dma((n_fsdp, 3)),
            dma((n_fsdp, 3)),
            dma((s,)),
            dma((s,)),
            dma((3,)),
            dma((3,)),
            dma((4,)),
            dma((4,)),
        ],
        compiler_params=pltpu.CompilerParams(
            collective_id=0, has_side_effects=True, vmem_limit_bytes=48 * 2**20
        ),
        cost_estimate=pl.CostEstimate(
            flops=6 * tok * width * cols, bytes_accessed=4 * tok * width, transcendentals=0
        ),
    )(acts, cotangent, inner_weight)


def by_collectives(acts, cotangent, inner_weight):
    width = acts.shape[1]
    scale = 1.0 / width**0.5
    gathered = lax.all_gather(inner_weight, "fsdp", axis=0, tiled=True)
    pre = jnp.dot(acts, gathered, preferred_element_type=jnp.float32) * scale
    sig = jax.nn.sigmoid(pre)
    grad_pre = (cotangent.astype(jnp.float32) * sig * (1.0 + pre * (1.0 - sig))).astype(
        jnp.bfloat16
    )
    input_grad = (jnp.dot(grad_pre, gathered.T, preferred_element_type=jnp.float32) * scale).astype(
        jnp.bfloat16
    )
    term = contract_rows(acts, grad_pre) * scale
    weight_grad = lax.psum_scatter(
        term.astype(jnp.bfloat16), "fsdp", scatter_dimension=0, tiled=True
    ).astype(jnp.float32)
    return input_grad, lax.psum(weight_grad, "replica")


def per_device(acts, cotangent, inner_weight, outer_weight, momentum):
    replicas = lax.axis_size("replica")
    n_fsdp = lax.axis_size("fsdp")
    rows = inner_weight.shape[0]
    if replicas == 8 and rows % 256 == 0 and n_fsdp > 1:
        input_grad, grad_sum = fused(acts, cotangent, inner_weight, n_fsdp)
    else:
        input_grad, grad_sum = by_collectives(acts, cotangent, inner_weight)
    delta_mean = (outer_weight - inner_weight.astype(jnp.float32)) + (
        lr_inner / replicas
    ) * grad_sum.astype(jnp.float32)
    new_outer, new_momentum = outer_update(delta_mean, outer_weight, momentum)
    return (input_grad, new_outer, new_momentum, new_outer.astype(jnp.bfloat16))


def solution(mesh):
    placed = (
        P(("replica", "fsdp"), None),
        P(("replica", "fsdp"), None),
        P("fsdp", None),
        P("fsdp", None),
        P("fsdp", None),
    )
    return jax.shard_map(
        per_device,
        mesh=mesh,
        in_specs=placed,
        out_specs=(P(("replica", "fsdp"), None), P("fsdp", None), P("fsdp", None), P("fsdp", None)),
        check_vma=False,
    )
```

```python
import functools

import jax
import jax.numpy as jnp
from jax import lax
from jax.experimental import pallas as pl
from jax.experimental.pallas import tpu as pltpu
from jax.sharding import PartitionSpec as P

lr_inner = 4.0
beta = 0.9
lr_outer = 0.7

MESH = pl.DeviceIdType.MESH


def contract_rows(left, right):
    return lax.dot_general(
        left, right, (((0,), (0,)), ((), ())), preferred_element_type=jnp.float32
    )


def outer_update(delta_mean, outer_rows, moment_rows):
    moment_next = beta * moment_rows + delta_mean
    outer_next = outer_rows - lr_outer * (delta_mean + beta * moment_next)
    return (outer_next, moment_next)


def kernel(
    n_fsdp,
    acts_hbm,
    cot_hbm,
    w_hbm,
    ig_hbm,
    g_hbm,
    acts,
    cot,
    acts_t,
    w_all,
    ig,
    sib_out,
    sib_in,
    half_sum,
    first_out,
    first_in,
    second_out,
    second_in,
    shard_out,
    shard_in,
    total,
    local_sem,
    wz_s,
    wz_r,
    wp_s,
    wp_r,
    wc_s,
    wc_r,
    tc_s,
    tc_r,
    tp_s,
    tp_r,
    tz_s,
    tz_r,
    gp_s,
    gp_r,
    gc_s,
    gc_r,
):
    me = lax.axis_index("replica")
    z = lax.axis_index("fsdp")
    rows = w_hbm.shape[0]
    half = rows // 2
    sub = half // 4
    width = acts.shape[1]
    scale = 1.0 / width**0.5
    chip, core = me // 2, me % 2
    x, y = chip % 2, chip // 2
    chips = (y * 2 + 1 - x, (1 - y) * 2 + x, (1 - y) * 2 + 1 - x)
    sibling = (chip * 2 + 1 - core, z)
    peers = [(q * 2 + core, z) for q in chips]
    x_peer, y_peer, _ = peers
    hop = sub // 2
    near, two, mirror = z + 1 - 2 * (z % 2), (z + 2) % 4, 3 - z
    middle = (z + z // 2) % 2
    sources = (near, middle * mirror + (1 - middle) * two, middle * two + (1 - middle) * mirror)
    targets = (mirror, two, near, z)

    def at(ref, start, size):
        return ref.at[pl.ds(pl.multiple_of(start, 16), size)]

    def remote(src, dst, s, r, dev):
        return pltpu.make_async_remote_copy(
            src_ref=src, dst_ref=dst, send_sem=s, recv_sem=r, device_id=dev, device_id_type=MESH
        )

    loads = [
        pltpu.make_async_copy(w_hbm, at(w_all, z * rows, rows), local_sem.at[0]),
        pltpu.make_async_copy(acts_hbm, acts, local_sem.at[1]),
        pltpu.make_async_copy(cot_hbm, cot, local_sem.at[2]),
    ]
    for load in loads:
        load.start()

    barrier = pltpu.get_barrier_semaphore()
    partners = [(me, other) for other in targets[:3]] + peers + [sibling]
    for dev in partners:
        pl.semaphore_signal(barrier, inc=1, device_id=dev, device_id_type=MESH)
    pl.semaphore_wait(barrier, len(partners))

    sent = []

    def send(src, dst, s, r, dev):
        copy = remote(src, dst, s, r, dev)
        copy.start()
        sent.append(copy)

    def arrived(landing, s, r, dev):
        remote(landing, landing, s, r, dev).wait_recv()

    def hand_on(source, up, down, src):
        piece = at(w_all, source * rows + mine, sub)
        for way, (cond, other) in enumerate(((up, z + 1), (down, z - 1))):

            @pl.when(cond)
            def _():
                remote(
                    src, piece, wz_s.at[way, source], wz_r.at[source], (me, other)
                ).start()

    def handed_on(source, up, down):
        piece = at(w_all, source * rows + mine, sub)
        for way, (cond, other) in enumerate(((up, z + 1), (down, z - 1))):

            @pl.when(cond)
            def _():
                remote(
                    piece, piece, wz_s.at[way, source], wz_r.at[source], (me, other)
                ).wait_send()

    mine = core * half + chip * sub
    hand_on(z, z < n_fsdp - 1, z > 0, at(w_hbm, mine, sub))
    for load in loads:
        load.wait()

    def partial_pre(start, size):
        start = pl.multiple_of(start, 128)
        return jnp.dot(
            acts[:, pl.ds(start, size)],
            w_all[pl.ds(start, size), :],
            preferred_element_type=jnp.float32,
        )

    def onward(source):
        return jnp.logical_and(source < z, z < n_fsdp - 1), jnp.logical_and(source > z, z > 0)

    for t, source in enumerate(sources):
        piece = at(w_all, source * rows + mine, sub)
        arrived(piece, wz_s.at[0, source], wz_r.at[source], (me, near))
        hand_on(source, *onward(source), piece)
        send(piece, piece, wp_s.at[t, 0], wp_r.at[t, 0], x_peer)
        send(piece, piece, wp_s.at[t, 1], wp_r.at[t, 1], y_peer)

    pre = partial_pre(z * rows, rows)

    def relay(t):
        start = sources[t] * rows + core * half
        arrived(at(w_all, start + chips[0] * sub, sub), wp_s.at[t, 0], wp_r.at[t, 0], x_peer)
        piece = at(w_all, start + chips[0] * sub, hop)
        send(piece, piece, wp_s.at[t, 3], wp_r.at[t, 3], y_peer)
        arrived(at(w_all, start + chips[1] * sub, sub), wp_s.at[t, 1], wp_r.at[t, 1], y_peer)
        piece = at(w_all, start + chips[1] * sub + hop, hop)
        send(piece, piece, wp_s.at[t, 2], wp_r.at[t, 2], x_peer)

    def use(t):
        start = sources[t] * rows + core * half
        diagonal = start + chips[2] * sub
        arrived(at(w_all, diagonal, hop), wp_s.at[t, 3], wp_r.at[t, 3], y_peer)
        arrived(at(w_all, diagonal + hop, hop), wp_s.at[t, 2], wp_r.at[t, 2], x_peer)
        piece = at(w_all, start, half)
        send(piece, piece, wc_s.at[t], wc_r.at[t], sibling)
        return partial_pre(start, half)

    relay(0)
    for b in range(width // half):
        acts_t[b * half : (b + 1) * half, :] = acts[:, b * half : (b + 1) * half].T
    relay(1)
    pre += use(0)
    relay(2)
    pre += use(1)
    pre += use(2)
    for t, source in enumerate(sources):
        start = source * rows + (1 - core) * half
        arrived(at(w_all, start, half), wc_s.at[t], wc_r.at[t], sibling)
        pre += partial_pre(start, half)

    pre = pre * scale
    sig = jax.nn.sigmoid(pre)
    grad_pre = (cot[...].astype(jnp.float32) * sig * (1.0 + pre * (1.0 - sig))).astype(
        jnp.bfloat16
    )

    def term(start):
        block = acts_t[pl.ds(pl.multiple_of(start, 128), half), :]
        return jnp.dot(block, grad_pre, preferred_element_type=jnp.float32) * scale

    for i, target in enumerate(targets):
        sib_out[i] = term(target * rows + (1 - core) * half).astype(jnp.bfloat16)
        send(sib_out.at[i], sib_in.at[i], tc_s.at[i], tc_r.at[i], sibling)

    def rows_of(i, q, second):
        return half_sum[i, pl.ds(pl.multiple_of(q * sub + second * hop, 16), hop), :]

    def to_plane(i):
        own = term(targets[i] * rows + core * half)
        arrived(sib_in.at[i], tc_s.at[i], tc_r.at[i], sibling)
        half_sum[i] = own + sib_in[i].astype(jnp.float32)
        for k in range(2):
            first_out[i, k, :hop] = rows_of(i, chips[2], k).astype(jnp.bfloat16)
            first_out[i, k, hop:] = rows_of(i, chips[k], k).astype(jnp.bfloat16)
            send(
                first_out.at[i, k], first_in.at[i, k], tp_s.at[i, k], tp_r.at[i, k], peers[k]
            )

    def second(i):
        for k in range(2):
            arrived(first_in.at[i, k], tp_s.at[i, k], tp_r.at[i, k], peers[k])
            second_out[i, k] = (
                rows_of(i, chips[1 - k], k) + first_in[i, k, :hop].astype(jnp.float32)
            ).astype(jnp.bfloat16)
            send(
                second_out.at[i, k],
                second_in.at[i, k],
                tp_s.at[i, 2 + k],
                tp_r.at[i, 2 + k],
                peers[1 - k],
            )

    def third(i):
        parts = []
        for k in range(2):
            arrived(second_in.at[i, k], tp_s.at[i, 2 + k], tp_r.at[i, 2 + k], peers[1 - k])
            parts.append(
                rows_of(i, chip, k)
                + first_in[i, k, hop:].astype(jnp.float32)
                + second_in[i, k].astype(jnp.float32)
            )
        if i == n_fsdp - 1:
            return parts
        for k in range(2):
            shard_out[i, k * hop : (k + 1) * hop] = parts[k].astype(jnp.bfloat16)
        send(shard_out.at[i], shard_in.at[i], tz_s.at[i], tz_r.at[i], (me, targets[i]))

    stores = []

    def input_rows(i):
        c0, c1 = i * rows, (i + 1) * rows
        ig[:, c0:c1] = (
            lax.dot_general(
                grad_pre,
                w_all[c0:c1, :],
                (((1,), (1,)), ((), ())),
                preferred_element_type=jnp.float32,
            )
            * scale
        ).astype(jnp.bfloat16)
        store = pltpu.make_async_copy(
            ig.at[:, c0:c1], ig_hbm.at[:, c0:c1], local_sem.at[3 + i]
        )
        store.start()
        stores.append(store)

    for i in range(n_fsdp):
        to_plane(i)
    input_rows(0)
    second(0)
    input_rows(1)
    second(1)
    third(0)
    input_rows(2)
    second(2)
    third(1)
    input_rows(3)
    second(3)
    third(2)
    parts = third(3)
    for i in range(n_fsdp - 1):
        arrived(shard_in.at[i], tz_s.at[i], tz_r.at[i], (me, targets[i]))
        for k in range(2):
            parts[k] += shard_in[i, k * hop : (k + 1) * hop].astype(jnp.float32)

    for k in range(2):
        start = pl.multiple_of(mine + k * hop, 16)
        total[pl.ds(start, hop), :] = parts[k].astype(jnp.bfloat16)
    piece = at(total, mine, sub)
    for k in (2, 0, 1):
        send(piece, piece, gp_s.at[k], gp_r.at[k], peers[k])
    send(piece, piece, gc_s.at[3], gc_r.at[3], sibling)
    for k in range(3):
        piece = at(total, core * half + chips[k] * sub, sub)
        arrived(piece, gp_s.at[k], gp_r.at[k], peers[k])
        send(piece, piece, gc_s.at[k], gc_r.at[k], sibling)
    for k in (3, 0, 1, 2):
        q = chip if k == 3 else chips[k]
        arrived(at(total, (1 - core) * half + q * sub, sub), gc_s.at[k], gc_r.at[k], sibling)
    last = pltpu.make_async_copy(total, g_hbm, local_sem.at[3 + n_fsdp])
    last.start()
    for copy in sent:
        copy.wait_send()
    handed_on(z, z < n_fsdp - 1, z > 0)
    for source in sources:
        handed_on(source, *onward(source))
    for store in stores:
        store.wait()
    last.wait()


def fused(acts, cotangent, inner_weight, n_fsdp):
    tok, width = acts.shape
    rows, cols = inner_weight.shape
    half, sub = rows // 2, rows // 8
    bf = jnp.bfloat16
    dma = pltpu.SemaphoreType.DMA
    s = n_fsdp - 1
    anywhere = pl.BlockSpec(memory_space=pl.ANY)
    return pl.pallas_call(
        functools.partial(kernel, n_fsdp),
        out_shape=(
            jax.ShapeDtypeStruct((tok, width), bf),
            jax.ShapeDtypeStruct((rows, cols), bf),
        ),
        in_specs=[pl.BlockSpec(memory_space=pltpu.HBM)] * 3,
        out_specs=(anywhere, anywhere),
        scratch_shapes=[
            pltpu.VMEM((tok, width), bf),
            pltpu.VMEM((tok, cols), bf),
            pltpu.VMEM((width, tok), bf),
            pltpu.VMEM((width, cols), bf),
            pltpu.VMEM((tok, width), bf),
            pltpu.VMEM((n_fsdp, half, cols), bf),
            pltpu.VMEM((n_fsdp, half, cols), bf),
            pltpu.VMEM((n_fsdp, half, cols), jnp.float32),
            pltpu.VMEM((n_fsdp, 2, sub, cols), bf),
            pltpu.VMEM((n_fsdp, 2, sub, cols), bf),
            pltpu.VMEM((n_fsdp, 2, sub // 2, cols), bf),
            pltpu.VMEM((n_fsdp, 2, sub // 2, cols), bf),
            pltpu.VMEM((s, sub, cols), bf),
            pltpu.VMEM((s, sub, cols), bf),
            pltpu.VMEM((rows, cols), bf),
            dma((4 + n_fsdp,)),
            dma((2, n_fsdp)),
            dma((n_fsdp,)),
            dma((s, 4)),
            dma((s, 4)),
            dma((s,)),
            dma((s,)),
            dma((n_fsdp,)),
            dma((n_fsdp,)),
            dma((n_fsdp, 4)),
            dma((n_fsdp, 4)),
            dma((s,)),
            dma((s,)),
            dma((3,)),
            dma((3,)),
            dma((4,)),
            dma((4,)),
        ],
        compiler_params=pltpu.CompilerParams(
            collective_id=0, has_side_effects=True, vmem_limit_bytes=61 * 2**20
        ),
        cost_estimate=pl.CostEstimate(
            flops=6 * tok * width * cols, bytes_accessed=4 * tok * width, transcendentals=0
        ),
    )(acts, cotangent, inner_weight)


def by_collectives(acts, cotangent, inner_weight):
    width = acts.shape[1]
    scale = 1.0 / width**0.5
    gathered = lax.all_gather(inner_weight, "fsdp", axis=0, tiled=True)
    pre = jnp.dot(acts, gathered, preferred_element_type=jnp.float32) * scale
    sig = jax.nn.sigmoid(pre)
    grad_pre = (cotangent.astype(jnp.float32) * sig * (1.0 + pre * (1.0 - sig))).astype(
        jnp.bfloat16
    )
    input_grad = (jnp.dot(grad_pre, gathered.T, preferred_element_type=jnp.float32) * scale).astype(
        jnp.bfloat16
    )
    term = contract_rows(acts, grad_pre) * scale
    weight_grad = lax.psum_scatter(
        term.astype(jnp.bfloat16), "fsdp", scatter_dimension=0, tiled=True
    ).astype(jnp.float32)
    return input_grad, lax.psum(weight_grad, "replica")


def per_device(acts, cotangent, inner_weight, outer_weight, momentum):
    replicas = lax.axis_size("replica")
    n_fsdp = lax.axis_size("fsdp")
    rows = inner_weight.shape[0]
    if replicas == 8 and n_fsdp == 4 and rows % 256 == 0:
        input_grad, grad_sum = fused(acts, cotangent, inner_weight, n_fsdp)
    else:
        input_grad, grad_sum = by_collectives(acts, cotangent, inner_weight)
    delta_mean = (outer_weight - inner_weight.astype(jnp.float32)) + (
        lr_inner / replicas
    ) * grad_sum.astype(jnp.float32)
    new_outer, new_momentum = outer_update(delta_mean, outer_weight, momentum)
    return (input_grad, new_outer, new_momentum, new_outer.astype(jnp.bfloat16))


def solution(mesh):
    placed = (
        P(("replica", "fsdp"), None),
        P(("replica", "fsdp"), None),
        P("fsdp", None),
        P("fsdp", None),
        P("fsdp", None),
    )
    return jax.shard_map(
        per_device,
        mesh=mesh,
        in_specs=placed,
        out_specs=(P(("replica", "fsdp"), None), P("fsdp", None), P("fsdp", None), P("fsdp", None)),
        check_vma=False,
    )
```

```python
import functools

import jax
import jax.numpy as jnp
from jax import lax
from jax.experimental import pallas as pl
from jax.experimental.pallas import tpu as pltpu
from jax.sharding import PartitionSpec as P

lr_inner = 4.0
beta = 0.9
lr_outer = 0.7

MESH = pl.DeviceIdType.MESH


def contract_rows(left, right):
    return lax.dot_general(
        left, right, (((0,), (0,)), ((), ())), preferred_element_type=jnp.float32
    )


def outer_update(delta_mean, outer_rows, moment_rows):
    moment_next = beta * moment_rows + delta_mean
    outer_next = outer_rows - lr_outer * (delta_mean + beta * moment_next)
    return (outer_next, moment_next)


def kernel(
    n_fsdp,
    acts_hbm,
    cot_hbm,
    w_hbm,
    ig_hbm,
    g_hbm,
    acts,
    cot,
    acts_t,
    w_all,
    ig,
    sib_out,
    sib_in,
    half_sum,
    first_out,
    first_in,
    second_out,
    second_in,
    shard_out,
    shard_in,
    total,
    local_sem,
    wz_s,
    wz_r,
    wp_s,
    wp_r,
    wc_s,
    wc_r,
    tc_s,
    tc_r,
    tp_s,
    tp_r,
    tz_s,
    tz_r,
    gp_s,
    gp_r,
    gc_s,
    gc_r,
):
    me = lax.axis_index("replica")
    z = lax.axis_index("fsdp")
    rows = w_hbm.shape[0]
    half = rows // 2
    sub = half // 4
    width = acts.shape[1]
    scale = 1.0 / width**0.5
    chip, core = me // 2, me % 2
    x, y = chip % 2, chip // 2
    chips = (y * 2 + 1 - x, (1 - y) * 2 + x, (1 - y) * 2 + 1 - x)
    sibling = (chip * 2 + 1 - core, z)
    peers = [(q * 2 + core, z) for q in chips]
    x_peer, y_peer, _ = peers
    hop = sub // 2
    near, two, mirror = z + 1 - 2 * (z % 2), (z + 2) % 4, 3 - z
    middle = (z + z // 2) % 2
    sources = (near, middle * mirror + (1 - middle) * two, middle * two + (1 - middle) * mirror)
    targets = (mirror, two, near, z)

    def at(ref, start, size):
        return ref.at[pl.ds(pl.multiple_of(start, 16), size)]

    def remote(src, dst, s, r, dev):
        return pltpu.make_async_remote_copy(
            src_ref=src, dst_ref=dst, send_sem=s, recv_sem=r, device_id=dev, device_id_type=MESH
        )

    loads = [
        pltpu.make_async_copy(w_hbm, at(w_all, z * rows, rows), local_sem.at[0]),
        pltpu.make_async_copy(acts_hbm, acts, local_sem.at[1]),
        pltpu.make_async_copy(cot_hbm, cot, local_sem.at[2]),
    ]
    for load in loads:
        load.start()

    barrier = pltpu.get_barrier_semaphore()
    partners = [(me, other) for other in targets[:3]] + peers + [sibling]
    for dev in partners:
        pl.semaphore_signal(barrier, inc=1, device_id=dev, device_id_type=MESH)
    pl.semaphore_wait(barrier, len(partners))

    sent = []

    def send(src, dst, s, r, dev):
        copy = remote(src, dst, s, r, dev)
        copy.start()
        sent.append(copy)

    def arrived(landing, s, r, dev):
        remote(landing, landing, s, r, dev).wait_recv()

    def hand_on(source, up, down, src):
        piece = at(w_all, source * rows + mine, sub)
        for way, (cond, other) in enumerate(((up, z + 1), (down, z - 1))):

            @pl.when(cond)
            def _():
                remote(
                    src, piece, wz_s.at[way, source], wz_r.at[source], (me, other)
                ).start()

    def handed_on(source, up, down):
        piece = at(w_all, source * rows + mine, sub)
        for way, (cond, other) in enumerate(((up, z + 1), (down, z - 1))):

            @pl.when(cond)
            def _():
                remote(
                    piece, piece, wz_s.at[way, source], wz_r.at[source], (me, other)
                ).wait_send()

    mine = core * half + chip * sub
    hand_on(z, z < n_fsdp - 1, z > 0, at(w_hbm, mine, sub))

    def turn(b):
        acts_t[b * half : (b + 1) * half, :] = acts[:, b * half : (b + 1) * half].T

    loads[1].wait()
    turn(0)
    turn(1)

    def partial_pre(start, size):
        start = pl.multiple_of(start, 128)
        return jnp.dot(
            acts[:, pl.ds(start, size)],
            w_all[pl.ds(start, size), :],
            preferred_element_type=jnp.float32,
        )

    def onward(source):
        return jnp.logical_and(source < z, z < n_fsdp - 1), jnp.logical_and(source > z, z > 0)

    for t, source in enumerate(sources):
        piece = at(w_all, source * rows + mine, sub)
        arrived(piece, wz_s.at[0, source], wz_r.at[source], (me, near))
        hand_on(source, *onward(source), piece)
        send(piece, piece, wp_s.at[t, 0], wp_r.at[t, 0], x_peer)
        send(piece, piece, wp_s.at[t, 1], wp_r.at[t, 1], y_peer)
        turn(2 + t)

    def relay(t):
        start = sources[t] * rows + core * half
        arrived(at(w_all, start + chips[0] * sub, sub), wp_s.at[t, 0], wp_r.at[t, 0], x_peer)
        piece = at(w_all, start + chips[0] * sub, hop)
        send(piece, piece, wp_s.at[t, 3], wp_r.at[t, 3], y_peer)
        arrived(at(w_all, start + chips[1] * sub, sub), wp_s.at[t, 1], wp_r.at[t, 1], y_peer)
        piece = at(w_all, start + chips[1] * sub + hop, hop)
        send(piece, piece, wp_s.at[t, 2], wp_r.at[t, 2], x_peer)

    def use(t):
        start = sources[t] * rows + core * half
        diagonal = start + chips[2] * sub
        arrived(at(w_all, diagonal, hop), wp_s.at[t, 3], wp_r.at[t, 3], y_peer)
        arrived(at(w_all, diagonal + hop, hop), wp_s.at[t, 2], wp_r.at[t, 2], x_peer)
        piece = at(w_all, start, half)
        send(piece, piece, wc_s.at[t], wc_r.at[t], sibling)
        return partial_pre(start, half)

    loads[0].wait()
    loads[2].wait()
    relay(0)
    pre = partial_pre(z * rows, half)
    turn(5)
    relay(1)
    pre += use(0)
    pre += partial_pre(z * rows + half, half)
    for b in range(6, width // half):
        turn(b)
    relay(2)
    pre += use(1)
    pre += use(2)
    for t, source in enumerate(sources):
        start = source * rows + (1 - core) * half
        arrived(at(w_all, start, half), wc_s.at[t], wc_r.at[t], sibling)
        pre += partial_pre(start, half)

    pre = pre * scale
    sig = jax.nn.sigmoid(pre)
    grad_pre = (cot[...].astype(jnp.float32) * sig * (1.0 + pre * (1.0 - sig))).astype(
        jnp.bfloat16
    )

    def term(start):
        block = acts_t[pl.ds(pl.multiple_of(start, 128), half), :]
        return jnp.dot(block, grad_pre, preferred_element_type=jnp.float32) * scale

    for i, target in enumerate(targets):
        sib_out[i] = term(target * rows + (1 - core) * half).astype(jnp.bfloat16)
        send(sib_out.at[i], sib_in.at[i], tc_s.at[i], tc_r.at[i], sibling)

    def rows_of(i, q, second):
        return half_sum[i, pl.ds(pl.multiple_of(q * sub + second * hop, 16), hop), :]

    def to_plane(i):
        own = term(targets[i] * rows + core * half)
        arrived(sib_in.at[i], tc_s.at[i], tc_r.at[i], sibling)
        half_sum[i] = own + sib_in[i].astype(jnp.float32)
        for k in range(2):
            first_out[i, k, :hop] = rows_of(i, chips[2], k).astype(jnp.bfloat16)
            first_out[i, k, hop:] = rows_of(i, chips[k], k).astype(jnp.bfloat16)
            send(
                first_out.at[i, k], first_in.at[i, k], tp_s.at[i, k], tp_r.at[i, k], peers[k]
            )

    def second(i):
        for k in range(2):
            arrived(first_in.at[i, k], tp_s.at[i, k], tp_r.at[i, k], peers[k])
            second_out[i, k] = (
                rows_of(i, chips[1 - k], k) + first_in[i, k, :hop].astype(jnp.float32)
            ).astype(jnp.bfloat16)
            send(
                second_out.at[i, k],
                second_in.at[i, k],
                tp_s.at[i, 2 + k],
                tp_r.at[i, 2 + k],
                peers[1 - k],
            )

    def third(i):
        parts = []
        for k in range(2):
            arrived(second_in.at[i, k], tp_s.at[i, 2 + k], tp_r.at[i, 2 + k], peers[1 - k])
            parts.append(
                rows_of(i, chip, k)
                + first_in[i, k, hop:].astype(jnp.float32)
                + second_in[i, k].astype(jnp.float32)
            )
        if i == n_fsdp - 1:
            return parts
        for k in range(2):
            shard_out[i, k * hop : (k + 1) * hop] = parts[k].astype(jnp.bfloat16)
        send(shard_out.at[i], shard_in.at[i], tz_s.at[i], tz_r.at[i], (me, targets[i]))

    stores = []

    def input_rows(i):
        c0, c1 = i * half, (i + 1) * half
        ig[:, c0:c1] = (
            lax.dot_general(
                grad_pre,
                w_all[c0:c1, :],
                (((1,), (1,)), ((), ())),
                preferred_element_type=jnp.float32,
            )
            * scale
        ).astype(jnp.bfloat16)
        store = pltpu.make_async_copy(
            ig.at[:, c0:c1], ig_hbm.at[:, c0:c1], local_sem.at[3 + i]
        )
        store.start()
        stores.append(store)

    to_plane(0)
    to_plane(1)
    second(0)
    to_plane(2)
    second(1)
    third(0)
    to_plane(3)
    input_rows(0)
    second(2)
    third(1)
    input_rows(1)
    input_rows(2)
    second(3)
    third(2)
    input_rows(3)
    input_rows(4)
    parts = third(3)
    for i in range(n_fsdp - 1):
        arrived(shard_in.at[i], tz_s.at[i], tz_r.at[i], (me, targets[i]))
        for k in range(2):
            parts[k] += shard_in[i, k * hop : (k + 1) * hop].astype(jnp.float32)

    for k in range(2):
        start = pl.multiple_of(mine + k * hop, 16)
        total[pl.ds(start, hop), :] = parts[k].astype(jnp.bfloat16)
    piece = at(total, mine, sub)
    for k in (2, 0, 1):
        send(piece, piece, gp_s.at[k], gp_r.at[k], peers[k])
    send(piece, piece, gc_s.at[3], gc_r.at[3], sibling)

    def keep(slot, start):
        store = pltpu.make_async_copy(
            at(total, start, sub), at(g_hbm, start, sub), local_sem.at[3 + 8 + slot]
        )
        store.start()
        stores.append(store)

    keep(3, mine)
    for i in range(5, width // half):
        input_rows(i)
    for k in range(3):
        start = core * half + chips[k] * sub
        piece = at(total, start, sub)
        arrived(piece, gp_s.at[k], gp_r.at[k], peers[k])
        send(piece, piece, gc_s.at[k], gc_r.at[k], sibling)
        keep(k, start)
    for k in (3, 0, 1, 2):
        start = (1 - core) * half + (chip if k == 3 else chips[k]) * sub
        arrived(at(total, start, sub), gc_s.at[k], gc_r.at[k], sibling)
        keep(4 + k, start)
    for copy in sent:
        copy.wait_send()
    handed_on(z, z < n_fsdp - 1, z > 0)
    for source in sources:
        handed_on(source, *onward(source))
    for store in stores:
        store.wait()


def fused(acts, cotangent, inner_weight, n_fsdp):
    tok, width = acts.shape
    rows, cols = inner_weight.shape
    half, sub = rows // 2, rows // 8
    bf = jnp.bfloat16
    dma = pltpu.SemaphoreType.DMA
    s = n_fsdp - 1
    anywhere = pl.BlockSpec(memory_space=pl.ANY)
    return pl.pallas_call(
        functools.partial(kernel, n_fsdp),
        out_shape=(
            jax.ShapeDtypeStruct((tok, width), bf),
            jax.ShapeDtypeStruct((rows, cols), bf),
        ),
        in_specs=[pl.BlockSpec(memory_space=pltpu.HBM)] * 3,
        out_specs=(anywhere, anywhere),
        scratch_shapes=[
            pltpu.VMEM((tok, width), bf),
            pltpu.VMEM((tok, cols), bf),
            pltpu.VMEM((width, tok), bf),
            pltpu.VMEM((width, cols), bf),
            pltpu.VMEM((tok, width), bf),
            pltpu.VMEM((n_fsdp, half, cols), bf),
            pltpu.VMEM((n_fsdp, half, cols), bf),
            pltpu.VMEM((n_fsdp, half, cols), jnp.float32),
            pltpu.VMEM((n_fsdp, 2, sub, cols), bf),
            pltpu.VMEM((n_fsdp, 2, sub, cols), bf),
            pltpu.VMEM((n_fsdp, 2, sub // 2, cols), bf),
            pltpu.VMEM((n_fsdp, 2, sub // 2, cols), bf),
            pltpu.VMEM((s, sub, cols), bf),
            pltpu.VMEM((s, sub, cols), bf),
            pltpu.VMEM((rows, cols), bf),
            dma((3 + 8 + 8,)),
            dma((2, n_fsdp)),
            dma((n_fsdp,)),
            dma((s, 4)),
            dma((s, 4)),
            dma((s,)),
            dma((s,)),
            dma((n_fsdp,)),
            dma((n_fsdp,)),
            dma((n_fsdp, 4)),
            dma((n_fsdp, 4)),
            dma((s,)),
            dma((s,)),
            dma((3,)),
            dma((3,)),
            dma((4,)),
            dma((4,)),
        ],
        compiler_params=pltpu.CompilerParams(
            collective_id=0, has_side_effects=True, vmem_limit_bytes=59 * 2**20
        ),
        cost_estimate=pl.CostEstimate(
            flops=6 * tok * width * cols, bytes_accessed=4 * tok * width, transcendentals=0
        ),
    )(acts, cotangent, inner_weight)


def by_collectives(acts, cotangent, inner_weight):
    width = acts.shape[1]
    scale = 1.0 / width**0.5
    gathered = lax.all_gather(inner_weight, "fsdp", axis=0, tiled=True)
    pre = jnp.dot(acts, gathered, preferred_element_type=jnp.float32) * scale
    sig = jax.nn.sigmoid(pre)
    grad_pre = (cotangent.astype(jnp.float32) * sig * (1.0 + pre * (1.0 - sig))).astype(
        jnp.bfloat16
    )
    input_grad = (jnp.dot(grad_pre, gathered.T, preferred_element_type=jnp.float32) * scale).astype(
        jnp.bfloat16
    )
    term = contract_rows(acts, grad_pre) * scale
    weight_grad = lax.psum_scatter(
        term.astype(jnp.bfloat16), "fsdp", scatter_dimension=0, tiled=True
    ).astype(jnp.float32)
    return input_grad, lax.psum(weight_grad, "replica")


def per_device(acts, cotangent, inner_weight, outer_weight, momentum):
    replicas = lax.axis_size("replica")
    n_fsdp = lax.axis_size("fsdp")
    rows = inner_weight.shape[0]
    if replicas == 8 and n_fsdp == 4 and rows % 256 == 0:
        input_grad, grad_sum = fused(acts, cotangent, inner_weight, n_fsdp)
    else:
        input_grad, grad_sum = by_collectives(acts, cotangent, inner_weight)
    delta_mean = (outer_weight - inner_weight.astype(jnp.float32)) + (
        lr_inner / replicas
    ) * grad_sum.astype(jnp.float32)
    new_outer, new_momentum = outer_update(delta_mean, outer_weight, momentum)
    return (input_grad, new_outer, new_momentum, new_outer.astype(jnp.bfloat16))


def solution(mesh):
    placed = (
        P(("replica", "fsdp"), None),
        P(("replica", "fsdp"), None),
        P("fsdp", None),
        P("fsdp", None),
        P("fsdp", None),
    )
    return jax.shard_map(
        per_device,
        mesh=mesh,
        in_specs=placed,
        out_specs=(P(("replica", "fsdp"), None), P("fsdp", None), P("fsdp", None), P("fsdp", None)),
        check_vma=False,
    )
```

```python
import functools

import jax
import jax.numpy as jnp
from jax import lax
from jax.experimental import pallas as pl
from jax.experimental.pallas import tpu as pltpu
from jax.sharding import PartitionSpec as P

lr_inner = 4.0
beta = 0.9
lr_outer = 0.7

MESH = pl.DeviceIdType.MESH


def contract_rows(left, right):
    return lax.dot_general(
        left, right, (((0,), (0,)), ((), ())), preferred_element_type=jnp.float32
    )


def outer_update(delta_mean, outer_rows, moment_rows):
    moment_next = beta * moment_rows + delta_mean
    outer_next = outer_rows - lr_outer * (delta_mean + beta * moment_next)
    return (outer_next, moment_next)


def kernel(
    n_fsdp,
    acts_hbm,
    cot_hbm,
    w_hbm,
    ig_hbm,
    g_hbm,
    acts,
    cot,
    acts_t,
    w_all,
    ig,
    sib_out,
    sib_in,
    half_sum,
    first_out,
    first_in,
    second_out,
    second_in,
    shard_out,
    shard_in,
    total,
    local_sem,
    wz_s,
    wz_r,
    wp_s,
    wp_r,
    wc_s,
    wc_r,
    tc_s,
    tc_r,
    tp_s,
    tp_r,
    tz_s,
    tz_r,
    gp_s,
    gp_r,
    gc_s,
    gc_r,
):
    me = lax.axis_index("replica")
    z = lax.axis_index("fsdp")
    rows = w_hbm.shape[0]
    half = rows // 2
    sub = half // 4
    width = acts.shape[1]
    scale = 1.0 / width**0.5
    chip, core = me // 2, me % 2
    x, y = chip % 2, chip // 2
    chips = (y * 2 + 1 - x, (1 - y) * 2 + x, (1 - y) * 2 + 1 - x)
    sibling = (chip * 2 + 1 - core, z)
    peers = [(q * 2 + core, z) for q in chips]
    x_peer, y_peer, _ = peers
    hop = sub // 2
    near, two, mirror = z + 1 - 2 * (z % 2), (z + 2) % 4, 3 - z
    middle = (z + z // 2) % 2
    sources = (near, middle * mirror + (1 - middle) * two, middle * two + (1 - middle) * mirror)
    targets = (mirror, two, near, z)

    def at(ref, start, size):
        return ref.at[pl.ds(pl.multiple_of(start, 16), size)]

    def remote(src, dst, s, r, dev):
        return pltpu.make_async_remote_copy(
            src_ref=src, dst_ref=dst, send_sem=s, recv_sem=r, device_id=dev, device_id_type=MESH
        )

    loads = [
        pltpu.make_async_copy(w_hbm, at(w_all, z * rows, rows), local_sem.at[0]),
        pltpu.make_async_copy(acts_hbm, acts, local_sem.at[1]),
        pltpu.make_async_copy(cot_hbm, cot, local_sem.at[2]),
    ]
    for load in loads:
        load.start()

    barrier = pltpu.get_barrier_semaphore()
    partners = [(me, other) for other in targets[:3]] + peers + [sibling]
    for dev in partners:
        pl.semaphore_signal(barrier, inc=1, device_id=dev, device_id_type=MESH)
    pl.semaphore_wait(barrier, len(partners))

    sent = []

    def send(src, dst, s, r, dev):
        copy = remote(src, dst, s, r, dev)
        copy.start()
        sent.append(copy)

    def arrived(landing, s, r, dev):
        remote(landing, landing, s, r, dev).wait_recv()

    def hand_on(source, up, down, src):
        piece = at(w_all, source * rows + mine, sub)
        for way, (cond, other) in enumerate(((up, z + 1), (down, z - 1))):

            @pl.when(cond)
            def _():
                remote(
                    src, piece, wz_s.at[way, source], wz_r.at[source], (me, other)
                ).start()

    def handed_on(source, up, down):
        piece = at(w_all, source * rows + mine, sub)
        for way, (cond, other) in enumerate(((up, z + 1), (down, z - 1))):

            @pl.when(cond)
            def _():
                remote(
                    piece, piece, wz_s.at[way, source], wz_r.at[source], (me, other)
                ).wait_send()

    mine = core * half + chip * sub
    hand_on(z, z < n_fsdp - 1, z > 0, at(w_hbm, mine, sub))

    def turn(b):
        acts_t[b * half : (b + 1) * half, :] = acts[:, b * half : (b + 1) * half].T

    loads[1].wait()
    turn(0)
    turn(1)

    def partial_pre(start, size):
        start = pl.multiple_of(start, 128)
        return jnp.dot(
            acts[:, pl.ds(start, size)],
            w_all[pl.ds(start, size), :],
            preferred_element_type=jnp.float32,
        )

    def onward(source):
        return jnp.logical_and(source < z, z < n_fsdp - 1), jnp.logical_and(source > z, z > 0)

    for t, source in enumerate(sources):
        piece = at(w_all, source * rows + mine, sub)
        arrived(piece, wz_s.at[0, source], wz_r.at[source], (me, near))
        hand_on(source, *onward(source), piece)
        send(piece, piece, wp_s.at[t, 0], wp_r.at[t, 0], x_peer)
        send(piece, piece, wp_s.at[t, 1], wp_r.at[t, 1], y_peer)
        send(piece, piece, wc_s.at[t, 3], wc_r.at[t, 3], sibling)
        turn(2 + t)

    def relay(t):
        start = sources[t] * rows + core * half
        arrived(at(w_all, start + chips[0] * sub, sub), wp_s.at[t, 0], wp_r.at[t, 0], x_peer)
        piece = at(w_all, start + chips[0] * sub, hop)
        send(piece, piece, wp_s.at[t, 3], wp_r.at[t, 3], y_peer)
        arrived(at(w_all, start + chips[1] * sub, sub), wp_s.at[t, 1], wp_r.at[t, 1], y_peer)
        piece = at(w_all, start + chips[1] * sub + hop, hop)
        send(piece, piece, wp_s.at[t, 2], wp_r.at[t, 2], x_peer)

        for k in range(2):
            piece = at(w_all, start + chips[k] * sub, sub)
            send(piece, piece, wc_s.at[t, k], wc_r.at[t, k], sibling)

    def use(t):
        start = sources[t] * rows + core * half
        diagonal = start + chips[2] * sub
        arrived(at(w_all, diagonal, hop), wp_s.at[t, 3], wp_r.at[t, 3], y_peer)
        arrived(at(w_all, diagonal + hop, hop), wp_s.at[t, 2], wp_r.at[t, 2], x_peer)
        piece = at(w_all, diagonal, sub)
        send(piece, piece, wc_s.at[t, 2], wc_r.at[t, 2], sibling)
        return partial_pre(start, half)

    def other_half(t):
        start = sources[t] * rows + (1 - core) * half
        for k, q in ((3, chip), (0, chips[0]), (1, chips[1]), (2, chips[2])):
            piece = at(w_all, start + q * sub, sub)
            arrived(piece, wc_s.at[t, k], wc_r.at[t, k], sibling)
        return partial_pre(start, half)

    loads[0].wait()
    loads[2].wait()
    relay(0)
    pre = partial_pre(z * rows, half)
    turn(5)
    relay(1)
    pre += use(0)
    pre += partial_pre(z * rows + half, half)
    for b in range(6, width // half):
        turn(b)
    relay(2)
    pre += use(1)
    pre += other_half(0)
    pre += use(2)
    pre += other_half(1)
    pre += other_half(2)

    pre = pre * scale
    sig = jax.nn.sigmoid(pre)
    grad_pre = (cot[...].astype(jnp.float32) * sig * (1.0 + pre * (1.0 - sig))).astype(
        jnp.bfloat16
    )

    def term(start):
        block = acts_t[pl.ds(pl.multiple_of(start, 128), half), :]
        return jnp.dot(block, grad_pre, preferred_element_type=jnp.float32) * scale

    def to_sibling(i):
        sib_out[i] = term(targets[i] * rows + (1 - core) * half).astype(jnp.bfloat16)
        send(sib_out.at[i], sib_in.at[i], tc_s.at[i], tc_r.at[i], sibling)

    def rows_of(i, q, second):
        return half_sum[i, pl.ds(pl.multiple_of(q * sub + second * hop, 16), hop), :]

    def to_plane(i):
        own = term(targets[i] * rows + core * half)
        arrived(sib_in.at[i], tc_s.at[i], tc_r.at[i], sibling)
        half_sum[i] = own + sib_in[i].astype(jnp.float32)
        for k in range(2):
            first_out[i, k, :hop] = rows_of(i, chips[2], k).astype(jnp.bfloat16)
            first_out[i, k, hop:] = rows_of(i, chips[k], k).astype(jnp.bfloat16)
            send(
                first_out.at[i, k], first_in.at[i, k], tp_s.at[i, k], tp_r.at[i, k], peers[k]
            )

    def second(i):
        for k in range(2):
            arrived(first_in.at[i, k], tp_s.at[i, k], tp_r.at[i, k], peers[k])
            second_out[i, k] = (
                rows_of(i, chips[1 - k], k) + first_in[i, k, :hop].astype(jnp.float32)
            ).astype(jnp.bfloat16)
            send(
                second_out.at[i, k],
                second_in.at[i, k],
                tp_s.at[i, 2 + k],
                tp_r.at[i, 2 + k],
                peers[1 - k],
            )

    def third(i):
        parts = []
        for k in range(2):
            arrived(second_in.at[i, k], tp_s.at[i, 2 + k], tp_r.at[i, 2 + k], peers[1 - k])
            parts.append(
                rows_of(i, chip, k)
                + first_in[i, k, hop:].astype(jnp.float32)
                + second_in[i, k].astype(jnp.float32)
            )
        if i == n_fsdp - 1:
            return parts
        for k in range(2):
            shard_out[i, k * hop : (k + 1) * hop] = parts[k].astype(jnp.bfloat16)
        send(shard_out.at[i], shard_in.at[i], tz_s.at[i], tz_r.at[i], (me, targets[i]))

    stores = []

    def input_rows(i):
        c0, c1 = i * half, (i + 1) * half
        ig[:, c0:c1] = (
            lax.dot_general(
                grad_pre,
                w_all[c0:c1, :],
                (((1,), (1,)), ((), ())),
                preferred_element_type=jnp.float32,
            )
            * scale
        ).astype(jnp.bfloat16)
        store = pltpu.make_async_copy(
            ig.at[:, c0:c1], ig_hbm.at[:, c0:c1], local_sem.at[3 + i]
        )
        store.start()
        stores.append(store)

    to_sibling(0)
    to_sibling(1)
    to_plane(0)
    to_sibling(2)
    to_plane(1)
    to_sibling(3)
    second(0)
    to_plane(2)
    second(1)
    third(0)
    to_plane(3)
    input_rows(0)
    second(2)
    third(1)
    input_rows(1)
    input_rows(2)
    second(3)
    third(2)
    input_rows(3)
    input_rows(4)
    parts = third(3)
    for i in range(n_fsdp - 1):
        arrived(shard_in.at[i], tz_s.at[i], tz_r.at[i], (me, targets[i]))
        for k in range(2):
            parts[k] += shard_in[i, k * hop : (k + 1) * hop].astype(jnp.float32)

    for k in range(2):
        start = pl.multiple_of(mine + k * hop, 16)
        total[pl.ds(start, hop), :] = parts[k].astype(jnp.bfloat16)
    piece = at(total, mine, sub)
    for k in (2, 0, 1):
        send(piece, piece, gp_s.at[k], gp_r.at[k], peers[k])
    send(piece, piece, gc_s.at[3], gc_r.at[3], sibling)

    def keep(slot, start):
        store = pltpu.make_async_copy(
            at(total, start, sub), at(g_hbm, start, sub), local_sem.at[3 + 8 + slot]
        )
        store.start()
        stores.append(store)

    keep(3, mine)
    for i in range(5, width // half):
        input_rows(i)
    for k in range(3):
        start = core * half + chips[k] * sub
        piece = at(total, start, sub)
        arrived(piece, gp_s.at[k], gp_r.at[k], peers[k])
        send(piece, piece, gc_s.at[k], gc_r.at[k], sibling)
        keep(k, start)
    for k in (3, 0, 1, 2):
        start = (1 - core) * half + (chip if k == 3 else chips[k]) * sub
        arrived(at(total, start, sub), gc_s.at[k], gc_r.at[k], sibling)
        keep(4 + k, start)
    for copy in sent:
        copy.wait_send()
    handed_on(z, z < n_fsdp - 1, z > 0)
    for source in sources:
        handed_on(source, *onward(source))
    for store in stores:
        store.wait()


def fused(acts, cotangent, inner_weight, n_fsdp):
    tok, width = acts.shape
    rows, cols = inner_weight.shape
    half, sub = rows // 2, rows // 8
    bf = jnp.bfloat16
    dma = pltpu.SemaphoreType.DMA
    s = n_fsdp - 1
    anywhere = pl.BlockSpec(memory_space=pl.ANY)
    return pl.pallas_call(
        functools.partial(kernel, n_fsdp),
        out_shape=(
            jax.ShapeDtypeStruct((tok, width), bf),
            jax.ShapeDtypeStruct((rows, cols), bf),
        ),
        in_specs=[pl.BlockSpec(memory_space=pltpu.HBM)] * 3,
        out_specs=(anywhere, anywhere),
        scratch_shapes=[
            pltpu.VMEM((tok, width), bf),
            pltpu.VMEM((tok, cols), bf),
            pltpu.VMEM((width, tok), bf),
            pltpu.VMEM((width, cols), bf),
            pltpu.VMEM((tok, width), bf),
            pltpu.VMEM((n_fsdp, half, cols), bf),
            pltpu.VMEM((n_fsdp, half, cols), bf),
            pltpu.VMEM((n_fsdp, half, cols), jnp.float32),
            pltpu.VMEM((n_fsdp, 2, sub, cols), bf),
            pltpu.VMEM((n_fsdp, 2, sub, cols), bf),
            pltpu.VMEM((n_fsdp, 2, sub // 2, cols), bf),
            pltpu.VMEM((n_fsdp, 2, sub // 2, cols), bf),
            pltpu.VMEM((s, sub, cols), bf),
            pltpu.VMEM((s, sub, cols), bf),
            pltpu.VMEM((rows, cols), bf),
            dma((3 + 8 + 8,)),
            dma((2, n_fsdp)),
            dma((n_fsdp,)),
            dma((s, 4)),
            dma((s, 4)),
            dma((s, 4)),
            dma((s, 4)),
            dma((n_fsdp,)),
            dma((n_fsdp,)),
            dma((n_fsdp, 4)),
            dma((n_fsdp, 4)),
            dma((s,)),
            dma((s,)),
            dma((3,)),
            dma((3,)),
            dma((4,)),
            dma((4,)),
        ],
        compiler_params=pltpu.CompilerParams(
            collective_id=0, has_side_effects=True, vmem_limit_bytes=59 * 2**20
        ),
        cost_estimate=pl.CostEstimate(
            flops=6 * tok * width * cols, bytes_accessed=4 * tok * width, transcendentals=0
        ),
    )(acts, cotangent, inner_weight)


def by_collectives(acts, cotangent, inner_weight):
    width = acts.shape[1]
    scale = 1.0 / width**0.5
    gathered = lax.all_gather(inner_weight, "fsdp", axis=0, tiled=True)
    pre = jnp.dot(acts, gathered, preferred_element_type=jnp.float32) * scale
    sig = jax.nn.sigmoid(pre)
    grad_pre = (cotangent.astype(jnp.float32) * sig * (1.0 + pre * (1.0 - sig))).astype(
        jnp.bfloat16
    )
    input_grad = (jnp.dot(grad_pre, gathered.T, preferred_element_type=jnp.float32) * scale).astype(
        jnp.bfloat16
    )
    term = contract_rows(acts, grad_pre) * scale
    weight_grad = lax.psum_scatter(
        term.astype(jnp.bfloat16), "fsdp", scatter_dimension=0, tiled=True
    ).astype(jnp.float32)
    return input_grad, lax.psum(weight_grad, "replica")


def per_device(acts, cotangent, inner_weight, outer_weight, momentum):
    replicas = lax.axis_size("replica")
    n_fsdp = lax.axis_size("fsdp")
    rows = inner_weight.shape[0]
    if replicas == 8 and n_fsdp == 4 and rows % 256 == 0:
        input_grad, grad_sum = fused(acts, cotangent, inner_weight, n_fsdp)
    else:
        input_grad, grad_sum = by_collectives(acts, cotangent, inner_weight)
    delta_mean = (outer_weight - inner_weight.astype(jnp.float32)) + (
        lr_inner / replicas
    ) * grad_sum.astype(jnp.float32)
    new_outer, new_momentum = outer_update(delta_mean, outer_weight, momentum)
    return (input_grad, new_outer, new_momentum, new_outer.astype(jnp.bfloat16))


def solution(mesh):
    placed = (
        P(("replica", "fsdp"), None),
        P(("replica", "fsdp"), None),
        P("fsdp", None),
        P("fsdp", None),
        P("fsdp", None),
    )
    return jax.shard_map(
        per_device,
        mesh=mesh,
        in_specs=placed,
        out_specs=(P(("replica", "fsdp"), None), P("fsdp", None), P("fsdp", None), P("fsdp", None)),
        check_vma=False,
    )
```
